512 devices in a mesh: row: 128 (over z, y, x_hi), head: 4 (over x_lo, core).
Axes of the slice: x: 4 (x_hi: 2, x_lo: 2; x = x_hi * 2 + x_lo), y: 4, z: 16, core: 2. Of those that a mesh axis runs over, the one named last changes fastest.
Arguments:
- pair_rep: float32 [512, 512, 128], P('row'), may hold values from -6 to 6
- residue_mask: int32 [512], replicated, may hold values 0 or 1
- chain_ids: int32 [512], replicated, may hold values from 0 to 5, never falling along the last dimension, each value on 1 to 170 neighbouring positions
- ln_gain: float32 [2, 128], replicated, may hold values from 0.5 to 1.5
- ln_shift: float32 [2, 128], replicated, may hold values from -4 to 4
- w_proj: float32 [2, 128, 4, 128], P(None, None, 'head'), may hold values from -0.5 to 0.5
- w_bias: float32 [2, 128, 4], P(None, None, 'head'), may hold values from -20 to 20
- chain_bias: float32 [2, 4], P(None, 'head'), may hold values from -2 to 2
- w_out: float32 [2, 128, 128], replicated, may hold values from -0.5 to 0.5
Outputs:
- paired: float32 [512, 512, 128], P(None, 'row')
The draws below stay inside these ranges and needn't reach their ends.
Inputs may be any that keep to these rules, and one draw needn't show every extreme that they name: `chain_ids`: chain numbers never fall from one token to the next.
All inputs are finite; a program needn't handle non-finite values.
Results may differ from the reference program's by a relative error of at most 0.00035.
Values sent between devices are 32-bit elements; how exact they have to be, the bound alone decides.
A program may use at most 64 MiB of HBM per device.

```python
import math
import jax
import jax.numpy as jnp
import numpy as np
from jax import lax

PAIR_CH = 128
HEADS = 4
HEAD_DIM = 32
CHAINS = 6
TOKENS = 512


def draw_pair_rep(key, part):
    key = jax.random.fold_in(key, 3)
    first_key = jax.random.fold_in(key, 0)
    base_field = jax.random.normal(first_key, (TOKENS, TOKENS, PAIR_CH), jnp.float32)
    return jnp.clip(base_field, -6.0, 6.0)


def draw_w_bias(key, part):
    key = jax.random.fold_in(key, 5)
    base_weight = jax.random.normal(key, (2, PAIR_CH, HEADS), jnp.float32) / math.sqrt(PAIR_CH)
    return jnp.clip(base_weight, -20.0, 20.0)


def place_ends(drawn, rng, smallest, high):
    extent = drawn.shape
    index_at = [jax.random.randint(jax.random.fold_in(rng, axis), (), 0, extent[axis]) for axis in range(len(extent))]
    drawn = drawn.at[tuple(index_at)].set(smallest)
    longest = extent.index(max(extent))
    index_at[longest] = (index_at[longest] + 1) % extent[longest]
    return drawn.at[tuple(index_at)].set(high)


def block_scale(key, extent, cuts, least, high):
    def one(position, shards_of):
        heights = jax.random.uniform(jax.random.fold_in(jax.random.fold_in(key, 6), position), (shards_of,), jnp.float32, least / len(cuts), high / len(cuts))
        return jnp.repeat(jnp.exp(heights), extent[position] // shards_of).reshape((-1,) + (1,) * (len(extent) - position - 1))

    factor_of = one(*cuts[0])
    for cut in cuts[1:]:
        factor_of = factor_of * one(*cut)
    return factor_of


def profile(count, total, bound, slope):
    portions = [(1 << 20) // math.isqrt(rank ** slope) + 1 for rank in range(2, count + 1)]
    spare, counts = total - bound - (count - 1), [1] * (count - 1)
    while spare > 0:
        candidates = [i for i in range(count - 1) if counts[i] < bound]
        whole, budget = sum([portions[i] for i in candidates]), spare
        for i in candidates:
            extra = min(bound - counts[i], max(1, budget * portions[i] // whole), spare)
            counts[i] = counts[i] + extra
            spare = spare - extra
    return np.array([bound] + counts)


def ragged_sizes(rng, amount, total, most, skew):
    if amount == 2:
        one = jax.random.randint(rng, (), max(1, total - most), min(most, total - 1) + 1)
        return jnp.stack([one, total - one])
    lengths = jnp.asarray(profile(amount, total, most, skew), jnp.int32)
    pairs = (amount - 1) // 2
    donor, sink = lengths[1:1 + 2 * pairs:2], lengths[2:2 + 2 * pairs:2]
    margin = jnp.minimum(donor - 1, most - sink)
    moved = jax.random.randint(jax.random.fold_in(rng, 1), (pairs,), 0, 1 << 20) % (margin + 1)
    lengths = lengths.at[1:1 + 2 * pairs:2].set(donor - moved).at[2:2 + 2 * pairs:2].set(sink + moved)
    return lengths[jax.random.permutation(jax.random.fold_in(rng, 2), amount)]


def bell_draw(key, extent, scale, reach, pieces=(), dtype=jnp.bfloat16):
    level = block_scale(key, extent, pieces, -0.22, 0.18) if pieces else 1.0
    drawn = jax.random.normal(key, extent, jnp.float32) * scale * level
    return jnp.minimum(jnp.maximum(drawn, -reach), reach).astype(dtype)


def setup_inputs(seed: int = 0) -> dict:
    key_of = jax.random.split(jax.random.key(seed), 10)
    return {
        "pair_rep": draw_pair_rep(jax.random.fold_in(key_of[9], 71), 0),
        "residue_mask": place_ends((jax.random.randint(key_of[1], (TOKENS,), 0, 8) < 7).astype(jnp.int32), jax.random.fold_in(key_of[1], 1), 0, 1),
        "chain_ids": jnp.searchsorted(jnp.cumsum(ragged_sizes(key_of[2], CHAINS, TOKENS, TOKENS // 3, 0)), jnp.arange(TOKENS), side="right").astype(jnp.int32),
        "ln_gain": jnp.clip(1.0 + 0.1 * jax.random.normal(key_of[3], (2, PAIR_CH), jnp.float32), 0.5, 1.5),
        "ln_shift": bell_draw(key_of[4], (2, PAIR_CH), 0.3, 4.0, (), jnp.float32),
        "w_proj": bell_draw(key_of[5], (2, PAIR_CH, HEADS, 4 * HEAD_DIM), PAIR_CH ** -0.5, 0.5, ((2, 4),), jnp.float32),
        "w_bias": draw_w_bias(jax.random.fold_in(key_of[9], 71), 0),
        "chain_bias": jnp.clip(jax.random.uniform(key_of[7], (2, HEADS), jnp.float32, -2.0, 2.0) * block_scale(key_of[7], (2, HEADS), ((1, 4),), -0.4, 0.0), -2.0, 2.0),
        "w_out": bell_draw(key_of[8], (2, HEADS * HEAD_DIM, PAIR_CH), (HEADS * HEAD_DIM) ** -0.5, 0.5, (), jnp.float32),
    }


highest = lax.Precision.HIGHEST

def normalize(features, scale_gain, shift_row):
    average = lax.optimization_barrier(jnp.mean(features, axis=-1, keepdims=True))
    centred = features - average
    spread = lax.optimization_barrier(jnp.mean(centred * centred, axis=-1, keepdims=True))
    return centred * lax.rsqrt(spread + 1e-05) * scale_gain + shift_row

def attend_rows(pair_rows, layer_idx, ln_gain, ln_shift, w_proj, w_bias, chain_bias, w_out, key_bias, same_chain):
    scale_gain = ln_gain[layer_idx]
    shift_row = ln_shift[layer_idx]
    proj_layer = w_proj[layer_idx]
    bias_layer = w_bias[layer_idx]
    out_layer = w_out[layer_idx]

    def plane_row(pair_row):
        normed = normalize(pair_row, scale_gain, shift_row)
        return jnp.einsum('kc,ch->hk', normed, bias_layer, precision=highest)
    planes = jnp.transpose(lax.map(plane_row, pair_rows), (1, 0, 2))
    planes = planes + chain_bias[layer_idx][:, None, None] * same_chain[None] + key_bias[None, None, :]
    inverse_root = 1.0 / math.sqrt(HEAD_DIM)

    def one_row(pair_row):
        normed = normalize(pair_row, scale_gain, shift_row)
        projected = jnp.einsum('nc,che->nhe', normed, proj_layer, precision=highest)
        queries = projected[..., :HEAD_DIM] * inverse_root
        keys_all = projected[..., HEAD_DIM:2 * HEAD_DIM]
        values_all = projected[..., 2 * HEAD_DIM:3 * HEAD_DIM]
        gate_vals = jax.nn.sigmoid(projected[..., 3 * HEAD_DIM:])
        scores = jnp.einsum('jhd,khd->hjk', queries, keys_all, precision=highest) + planes
        weights = jax.nn.softmax(scores, axis=-1)
        attended = jnp.einsum('hjk,khd->jhd', weights, values_all, precision=highest) * gate_vals
        flat = attended.reshape(TOKENS, HEADS * HEAD_DIM)
        return pair_row + jnp.dot(flat, out_layer, precision=highest)
    return lax.map(one_row, pair_rows)

def reference(pair_rep, residue_mask, chain_ids, ln_gain, ln_shift, w_proj, w_bias, chain_bias, w_out):
    key_bias = (residue_mask.astype(jnp.float32) - 1.0) * 1000000000.0
    same_chain = (chain_ids[:, None] == chain_ids[None, :]).astype(jnp.float32)
    after_start = attend_rows(pair_rep, 0, ln_gain, ln_shift, w_proj, w_bias, chain_bias, w_out, key_bias, same_chain)
    turned = jnp.transpose(after_start, (1, 0, 2))
    second = attend_rows(turned, 1, ln_gain, ln_shift, w_proj, w_bias, chain_bias, w_out, key_bias, same_chain)
    return jnp.transpose(second, (1, 0, 2))
```

```python
import functools
import math

import jax
import jax.numpy as jnp
from jax import lax
from jax.experimental import pallas as pl
from jax.experimental.pallas import tpu as pltpu
from jax.sharding import PartitionSpec as P

highest = lax.Precision.HIGHEST
MESH = pl.DeviceIdType.MESH
F32, BF16 = jnp.float32, jnp.bfloat16

GATHER = (0, 32)
PAIR_Z, PAIR_S = 64, 80
COL_CORE, COL_X, COL_FWD = 88, 96, 104
SMALL, W_CORE, W_X, W_FWD = 112, 116, 118, 120
OUT_CORE, OUT_X, OUT_FWD = 122, 126, 130
SLOTS = 134


def dot(a, b, dims, precision=None):
    return lax.dot_general(a, b, (dims, ((), ())), precision=precision, preferred_element_type=F32)


def split(x):
    high = x.astype(BF16)
    return high, (x - high.astype(F32)).astype(BF16)


def normalize(x, gain, shift):
    centred = x - jnp.mean(x, axis=-1, keepdims=True)
    spread = jnp.mean(centred * centred, axis=-1, keepdims=True)
    return centred * lax.rsqrt(spread + 1e-05) * gain + shift


def kernel(
    pair, mask, chain, ln_gain, ln_shift, w_own, wb_own, cb_own, w_out, out,
    xp, wp, small, plane0, plane1, after, mid, mid2, cols, k3, q3, vb, gates, bias, wall, marks, ss, rs,
):
    r, q = lax.axis_index("row"), lax.axis_index("head")
    z, s = r // 8, lax.rem(r, 8)
    y, xh = s // 2, lax.rem(s, 2)
    core, xlo = lax.rem(q, 2), q // 2
    other_core = (r, xlo * 2 + 1 - core)
    other_x = (r, (1 - xlo) * 2 + core)
    q_core, q_x = other_core[1], other_x[1]
    q_far = (1 - xlo) * 2 + 1 - core

    def at_z(k):
        return (lax.rem(z + k, 16) * 8 + s, q)

    def at_y(k):
        return (z * 8 + lax.rem(y + k, 4) * 2 + xh, q)

    def at_s(k):
        return (z * 8 + lax.rem(s + k, 8), q)

    at_x = (z * 8 + y * 2 + 1 - xh, q)

    def remote(src, dst, slot, device):
        return pltpu.make_async_remote_copy(
            src_ref=src, dst_ref=dst, send_sem=ss.at[slot], recv_sem=rs.at[slot],
            device_id=device, device_id_type=MESH,
        )

    def loop(low, high, body):
        def step(i, carry):
            body(i)
            return carry
        lax.fori_loop(low, high, step, 0)

    def far_first(i):
        j = (i + 1) // 2
        return 8 + j * (2 * lax.rem(i, 2) - 1)

    barrier = pltpu.get_barrier_semaphore()

    def greet(device):
        pl.semaphore_signal(barrier, inc=1, device_id=device, device_id_type=MESH)

    loop(1, 4, lambda k: greet((r, lax.rem(q + k, 4))))
    loop(1, 16, lambda k: greet(at_z(k)))
    loop(1, 8, lambda k: greet(at_s(k)))

    wp[q] = w_own[...]
    small[q] = jnp.concatenate(
        [wb_own[...], jnp.broadcast_to(cb_own[...], (2, 128)), jnp.zeros((4, 128), F32)], axis=0
    )

    def normed_row(a):
        return jnp.concatenate(
            [normalize(pair[a, pl.ds(t, 128, stride=4), :], ln_gain[0:1], ln_shift[0:1]) for t in range(4)], axis=0
        )

    own_normed = normed_row(q)
    pl.semaphore_wait(barrier, 25)

    loop(1, 4, lambda k: remote(small.at[q], small.at[q], SMALL + k, (r, lax.rem(q + k, 4))).start())
    for layer in range(2):
        remote(w_own.at[layer], wp.at[q, layer], W_CORE + layer, other_core).start()
        remote(w_own.at[layer], wp.at[q, layer], W_X + layer, other_x).start()

    def small_wait(k):
        owner = lax.rem(q + 4 - k, 4)
        copy = remote(small.at[owner], small.at[owner], SMALL + k, other_core)
        copy.wait_recv()
        copy.wait_send()

    loop(1, 4, small_wait)
    piece = dot(small[...].reshape(32, 128), own_normed, ((1,), (1,)), highest)
    for t in range(4):
        for h in range(4):
            plane0[z, y, xh, 4 * t + h : 4 * t + h + 1, :] = piece[8 * h : 8 * h + 1, 128 * t : 128 * t + 128]

    def gather_z(plane, base):
        def start(i):
            k = far_first(i)
            remote(plane.at[z, y, xh], plane.at[z, y, xh], base + k, at_z(k)).start()
        loop(0, 15, start)

    def gather_z_wait(plane, base):
        def wait(k):
            origin = lax.rem(z + 16 - k, 16)
            copy = remote(plane.at[origin, y, xh], plane.at[origin, y, xh], base + k, at_x)
            copy.wait_recv()
            copy.wait_send()
        loop(1, 16, wait)

    def gather_slab(plane, base):
        first, second = pl.ds(0, 8), pl.ds(8, 8)

        def y_first(yy, k, device):
            ref = plane.at[:, yy, xh, first]
            return remote(ref, ref, base + 16 + k, device)

        def x_first(xx):
            ref = plane.at[:, y, xx, second]
            return remote(ref, ref, base + 21, at_x)

        def y_second(yy, k, device):
            ref = plane.at[:, yy, :, second]
            return remote(ref, ref, base + 22 + k, device)

        def x_second(xx):
            ref = plane.at[:, :, xx, first]
            return remote(ref, ref, base + 20, at_x)

        x_first(xh).start()
        loop(1, 4, lambda k: y_first(y, k, at_y(k)).start())
        x_first(1 - xh).wait_recv()
        loop(1, 4, lambda k: y_second(y, k, at_y(k)).start())
        loop(1, 4, lambda k: y_first(lax.rem(y + 4 - k, 4), k, at_x).wait_recv())
        x_second(xh).start()
        loop(1, 4, lambda k: y_second(lax.rem(y + 4 - k, 4), k, at_x).wait_recv())
        x_second(1 - xh).wait_recv()
        loop(1, 4, lambda k: y_first(y, k, at_x).wait_send())
        loop(1, 4, lambda k: y_second(y, k, at_x).wait_send())
        x_first(xh).wait_send()
        x_second(xh).wait_send()

    gather_z(plane0, GATHER[0])

    for layer in range(2):
        remote(w_own.at[layer], wp.at[q_x, layer], W_X + layer, other_x).wait_recv()
        remote(wp.at[q_x, layer], wp.at[q_x, layer], W_FWD + layer, other_core).start()

    token = lax.broadcasted_iota(jnp.int32, (8, 512), 1)
    line = lax.broadcasted_iota(jnp.int32, (8, 512), 0)
    value = jnp.where(line < 4, chain[...].astype(F32), mask[...].astype(F32))
    value = jnp.where(lax.rem(token, 4) == lax.rem(line, 4), value, 0.0)
    place = lax.broadcasted_iota(jnp.int32, (512, 128), 0) // 4 == lax.broadcasted_iota(jnp.int32, (512, 128), 1)
    marks[...] = dot(value, place.astype(F32), ((1,), (0,)), highest)

    for layer in range(2):
        remote(w_own.at[layer], wp.at[q_core, layer], W_CORE + layer, other_core).wait_recv()
        remote(w_own.at[layer], wp.at[q_far, layer], W_FWD + layer, other_core).wait_recv()
        for slot, device in ((W_CORE, other_core), (W_X, other_x)):
            remote(w_own.at[layer], wp.at[q, layer], slot + layer, device).wait_send()
        remote(wp.at[q_x, layer], wp.at[q_x, layer], W_FWD + layer, other_core).wait_send()

    def weights(layer):
        for h in range(4):
            wall[pl.ds(128 * h, 128), :] = wp[h, layer].T

    def project(a, layer):
        normed = jnp.concatenate(
            [normalize(xp[a, t], ln_gain[layer : layer + 1], ln_shift[layer : layer + 1]) for t in range(4)], axis=0
        )
        normed_q = normalize(xp[a, q], ln_gain[layer : layer + 1], ln_shift[layer : layer + 1])
        for h in range(4):
            both = dot(wall[pl.ds(128 * h + 32, 64), :], normed, ((1,), (1,)), highest)
            key_high, key_low = split(both[0:32])
            k3[a, h] = jnp.concatenate([key_high, key_high, key_low], axis=0)
            value_high, value_low = split(both[32:64])
            vb[a, h] = jnp.concatenate([value_high, value_low, jnp.ones((16, 512), BF16)], axis=0)
            query = dot(wall[pl.ds(128 * h, 32), :], normed_q, ((1,), (1,)), highest) * (1.0 / math.sqrt(32))
            query_high, query_low = split(query)
            q3[a, h] = jnp.concatenate([query_high, query_low, query_high], axis=0)
            gates[a, pl.ds(32 * h, 32), :] = jax.nn.sigmoid(
                dot(wall[pl.ds(128 * h + 96, 32), :], normed_q, ((1,), (1,)), highest)
            )

    def make_bias(layer, plane):
        chain_q = jnp.broadcast_to(marks[pl.ds(q, 1), :], (128, 128)).T
        flat = plane.reshape(2048, 128)
        for t in range(4):
            same = (chain_q == marks[t : t + 1, :]).astype(F32)
            key_bias = (marks[4 + t : 5 + t, :] - 1.0) * 1000000000.0
            for h in range(4):
                tile = flat[pl.ds(4 * t + h, 128, stride=16), :]
                if layer == 1:
                    tile = tile.T
                bias[h, :, 128 * t : 128 * t + 128] = tile + small[h, 2 + layer : 3 + layer, :] * same + key_bias

    def attend(a, layer):
        heads = []
        for h in range(4):
            score = dot(q3[a, h], k3[a, h], ((0,), (0,))) + bias[h]
            weight = jnp.exp(score - jnp.max(score, axis=-1, keepdims=True))
            weight_high, weight_low = split(weight)
            total = dot(vb[a, h], weight_high, ((1,), (1,))) + dot(vb[a, h], weight_low, ((1,), (1,)))
            heads.append((total[0:32] + total[32:64]) / total[64:65] * gates[a, pl.ds(32 * h, 32), :])
        joined = jnp.concatenate(heads, axis=0)
        return xp[a, q] + dot(joined, w_out[layer], ((0,), (0,)), highest)

    def permute_row(a):
        for t in range(4):
            xp[a, t] = pair[a, pl.ds(t, 128, stride=4), :]

    weights(0)

    def first_project(a):
        permute_row(a)
        project(a, 0)

    loop(0, 4, first_project)
    gather_z_wait(plane0, GATHER[0])
    gather_slab(plane0, GATHER[0])
    make_bias(0, plane0)

    def first_attend(a):
        row = attend(a, 0)
        after[a] = row
        normed = normalize(row, ln_gain[1:2], ln_shift[1:2])
        mine = dot(small[...].reshape(32, 128), normed, ((1,), (1,)), highest)
        for h in range(4):
            plane1[z, y, xh, pl.ds(4 * a + h, 1), :] = mine[8 * h + 1 : 8 * h + 2, :]

    loop(0, 4, first_attend)

    def pair_z(i):
        k = far_first(i)
        there = lax.rem(z + k, 16)
        remote(after.at[:, pl.ds(pl.multiple_of(there * 8, 8), 8)], mid.at[:, z], PAIR_Z + k, at_z(k)).start()

    loop(0, 15, pair_z)
    gather_z(plane1, GATHER[1])
    mid[:, z] = after[:, pl.ds(pl.multiple_of(z * 8, 8), 8), :]
    weights(1)

    def pair_z_wait(k):
        origin = lax.rem(z + 16 - k, 16)
        copy = remote(after.at[:, pl.ds(0, 8)], mid.at[:, origin], PAIR_Z + k, at_x)
        copy.wait_recv()
        copy.wait_send()

    loop(1, 16, pair_z_wait)
    for a in range(4):
        flat_mid = mid.at[a].reshape(128, 128)
        for there in range(8):
            mid2[there, 16 * a : 16 * a + 16, :] = flat_mid[pl.ds(there, 16, stride=8), :]

    def pair_s(k):
        there = lax.rem(s + k, 8)
        remote(mid2.at[there], cols.at[q, s], PAIR_S + k, at_s(k)).start()

    loop(1, 8, pair_s)
    cols[q, s] = mid2[s]

    def share(origin):
        block = cols.at[q, origin]
        remote(block, block, COL_CORE + origin, other_core).start()
        remote(block, block, COL_X + origin, other_x).start()

    share(s)

    def pair_s_wait(k):
        origin = lax.rem(s + 8 - k, 8)
        copy = remote(mid2.at[0], cols.at[q, origin], PAIR_S + k, at_x)
        copy.wait_recv()
        copy.wait_send()
        share(origin)

    loop(1, 8, pair_s_wait)

    def pass_on(origin):
        block = cols.at[q_x, origin]
        remote(block, block, COL_X + origin, other_x).wait_recv()
        remote(block, block, COL_FWD + origin, other_core).start()

    loop(0, 8, pass_on)

    def permute_col(c):
        flat = cols.at[c].reshape(512, 128)
        for a in range(4):
            xp[c, a] = jnp.concatenate(
                [flat[pl.ds(16 * a + zz, 8, stride=64), :] for zz in range(16)], axis=0
            )

    def second_project(c):
        permute_col(c)
        project(c, 1)

    second_project(q)
    second_project(q_x)

    def share_wait(origin):
        block = cols.at[q, origin]
        remote(block, cols.at[q_core, origin], COL_CORE + origin, other_core).wait_recv()
        remote(block, block, COL_CORE + origin, other_core).wait_send()
        remote(block, block, COL_X + origin, other_x).wait_send()

    loop(0, 8, share_wait)
    second_project(q_core)

    def forward_wait(origin):
        block = cols.at[q_far, origin]
        remote(block, block, COL_FWD + origin, other_core).wait_recv()
        block = cols.at[q_x, origin]
        remote(block, block, COL_FWD + origin, other_core).wait_send()

    loop(0, 8, forward_wait)
    second_project(q_far)
    gather_z_wait(plane1, GATHER[1])
    gather_slab(plane1, GATHER[1])
    make_bias(1, plane1)

    def second_attend(c):
        out[c, q] = attend(c, 1)
        block = out.at[c, q]
        remote(block, block, OUT_X + c, other_x).start()
        remote(block, block, OUT_CORE + c, other_core).start()

    loop(0, 4, second_attend)

    def out_pass_on(c):
        block = out.at[c, q_x]
        remote(block, block, OUT_X + c, other_x).wait_recv()
        remote(block, block, OUT_FWD + c, other_core).start()

    loop(0, 4, out_pass_on)

    def out_wait(c):
        remote(out.at[c, q_core], out.at[c, q_core], OUT_CORE + c, other_core).wait_recv()
        remote(out.at[c, q_far], out.at[c, q_far], OUT_FWD + c, other_core).wait_recv()
        remote(out.at[c, q], out.at[c, q], OUT_X + c, other_x).wait_send()
        remote(out.at[c, q], out.at[c, q], OUT_CORE + c, other_core).wait_send()
        remote(out.at[c, q_x], out.at[c, q_x], OUT_FWD + c, other_core).wait_send()

    loop(0, 4, out_wait)


def shards(pair_rep, residue_mask, chain_ids, ln_gain, ln_shift, w_proj, w_bias, chain_bias, w_out):
    vmem = pl.BlockSpec(memory_space=pltpu.VMEM)
    result = pl.pallas_call(
        kernel,
        out_shape=jax.ShapeDtypeStruct((4, 4, 128, 128), F32),
        in_specs=[vmem] * 9,
        out_specs=vmem,
        scratch_shapes=[
            pltpu.VMEM((4, 4, 128, 128), F32),
            pltpu.VMEM((4, 2, 128, 128), F32),
            pltpu.VMEM((4, 8, 128), F32),
            pltpu.VMEM((16, 4, 2, 16, 128), F32),
            pltpu.VMEM((16, 4, 2, 16, 128), F32),
            pltpu.VMEM((4, 128, 128), F32),
            pltpu.VMEM((4, 16, 8, 128), F32),
            pltpu.VMEM((8, 64, 128), F32),
            pltpu.VMEM((4, 8, 64, 128), F32),
            pltpu.VMEM((4, 4, 96, 512), BF16),
            pltpu.VMEM((4, 4, 96, 128), BF16),
            pltpu.VMEM((4, 4, 80, 512), BF16),
            pltpu.VMEM((4, 128, 128), F32),
            pltpu.VMEM((4, 128, 512), F32),
            pltpu.VMEM((512, 128), F32),
            pltpu.VMEM((8, 128), F32),
            pltpu.SemaphoreType.DMA((SLOTS,)),
            pltpu.SemaphoreType.DMA((SLOTS,)),
        ],
        compiler_params=pltpu.CompilerParams(
            collective_id=0, has_side_effects=True, vmem_limit_bytes=40 * 1024 * 1024
        ),
    )(
        pair_rep,
        residue_mask.reshape(1, 512),
        chain_ids.reshape(1, 512),
        ln_gain,
        ln_shift,
        w_proj.reshape(2, 128, 128),
        w_bias.reshape(2, 128),
        chain_bias,
        w_out,
    )
    return jnp.transpose(result, (2, 1, 0, 3)).reshape(512, 4, 128)


def solution(mesh):
    in_specs = (
        P("row", None, None),
        P(),
        P(),
        P(),
        P(),
        P(None, None, "head", None),
        P(None, None, "head"),
        P(None, "head"),
        P(),
    )
    return jax.shard_map(shards, mesh=mesh, in_specs=in_specs, out_specs=P(None, "row", None), check_vma=False)
```

```python
import functools
import math

import jax
import jax.numpy as jnp
from jax import lax
from jax.experimental import pallas as pl
from jax.experimental.pallas import tpu as pltpu
from jax.sharding import PartitionSpec as P

highest = lax.Precision.HIGHEST
MESH = pl.DeviceIdType.MESH
F32, BF16 = jnp.float32, jnp.bfloat16

class Slots:
    def __init__(self):
        self.count = 0

    def take(self, number):
        self.count += number
        return self.count - number


arrive = Slots()
PLANE_Z = (arrive.take(4), arrive.take(8))
Y_FIRST, X_FIRST, Y_SECOND, X_SECOND = ([arrive.take(4) for _ in range(2)] for _ in range(4))
PAIR_Z, PAIR_S = arrive.take(4), arrive.take(4)
COL_CORE, COL_X, COL_FWD = arrive.take(4), arrive.take(4), arrive.take(4)
OUT_CORE, OUT_X, OUT_FWD = arrive.take(4), arrive.take(4), arrive.take(4)
SMALL, W_CORE, W_X, W_FWD = arrive.take(1), arrive.take(1), arrive.take(1), arrive.take(1)
LOCAL = OUT_CORE
leave = Slots()
LEFT_Z = (leave.take(1), leave.take(1))
LEFT_YX = (leave.take(1), leave.take(1))
LEFT_PAIR_Z, LEFT_PAIR_S, LEFT_COL, LEFT_OUT, LEFT_W, LEFT_SMALL = (leave.take(1) for _ in range(6))


def dot(a, b, dims, precision=None):
    return lax.dot_general(a, b, (dims, ((), ())), precision=precision, preferred_element_type=F32)


def split(x):
    high = x.astype(BF16)
    return high, (x - high.astype(F32)).astype(BF16)


def normalize(x, gain, shift):
    centred = x - jnp.mean(x, axis=-1, keepdims=True)
    spread = jnp.mean(centred * centred, axis=-1, keepdims=True)
    return centred * lax.rsqrt(spread + 1e-05) * gain + shift


def kernel(
    pair_in, mask_in, chain_in, gain_in, shift_in, w_own, wb_in, cb_in, w_out_in, out,
    pair, mask, chain, ln_gain, ln_shift, wb_own, cb_own, w_out,
    xp, wp, small, plane0, plane1, after, mid, mid2, cols, k3, q3, vb, gates, bias, wkv, wqg, marks, outs, ss, rs,
):
    r, q = lax.axis_index("row"), lax.axis_index("head")
    z, s = r // 8, lax.rem(r, 8)
    y, xh = s // 2, lax.rem(s, 2)
    core, xlo = lax.rem(q, 2), q // 2
    other_core = (r, xlo * 2 + 1 - core)
    other_x = (r, (1 - xlo) * 2 + core)
    q_core, q_x = other_core[1], other_x[1]
    q_far = (1 - xlo) * 2 + 1 - core

    def at_z(k):
        return (lax.rem(z + k, 16) * 8 + s, q)

    def at_y(k):
        return (z * 8 + lax.rem(y + k, 4) * 2 + xh, q)

    def at_s(k):
        return (z * 8 + lax.rem(s + k, 8), q)

    at_x = (z * 8 + y * 2 + 1 - xh, q)

    def send(src, dst, left, slot, device):
        pltpu.make_async_remote_copy(
            src_ref=src, dst_ref=dst, send_sem=ss.at[left], recv_sem=rs.at[slot],
            device_id=device, device_id_type=MESH,
        ).start()

    def arrived(ref, slot):
        pltpu.make_async_remote_copy(
            src_ref=ref, dst_ref=ref, send_sem=ss.at[0], recv_sem=rs.at[slot],
            device_id=at_x, device_id_type=MESH,
        ).wait_recv()

    def left(ref, slot):
        pltpu.make_async_remote_copy(
            src_ref=ref, dst_ref=ref, send_sem=ss.at[slot], recv_sem=rs.at[0],
            device_id=at_x, device_id_type=MESH,
        ).wait_send()

    def loop(low, high, body):
        def step(i, carry):
            body(i)
            return carry
        lax.fori_loop(low, high, step, 0)

    def far_first(i):
        j = (i + 1) // 2
        return 8 + j * (2 * lax.rem(i, 2) - 1)

    local = [
        pltpu.make_async_copy(pair_in.at[q], pair.at[q], rs.at[LOCAL]),
        pltpu.make_async_copy(gain_in, ln_gain, rs.at[LOCAL + 1]),
        pltpu.make_async_copy(shift_in, ln_shift, rs.at[LOCAL + 2]),
        pltpu.make_async_copy(wb_in, wb_own, rs.at[LOCAL + 3]),
        pltpu.make_async_copy(cb_in, cb_own, rs.at[LOCAL + 4]),
        pltpu.make_async_copy(w_own, wp.at[q], rs.at[LOCAL + 5]),
        pltpu.make_async_copy(mask_in, mask, rs.at[LOCAL + 6]),
        pltpu.make_async_copy(chain_in, chain, rs.at[LOCAL + 7]),
        pltpu.make_async_copy(w_out_in, w_out, rs.at[LOCAL + 8]),
    ] + [
        pltpu.make_async_copy(
            pair_in.at[lax.rem(q + k, 4)], pair.at[lax.rem(q + k, 4)], rs.at[LOCAL + 8 + k]
        )
        for k in range(1, 4)
    ]
    for copy in local[:6]:
        copy.start()

    barrier = pltpu.get_barrier_semaphore()

    def greet(device):
        pl.semaphore_signal(barrier, inc=1, device_id=device, device_id_type=MESH)

    loop(1, 4, lambda k: greet((r, lax.rem(q + k, 4))))
    loop(0, 15, lambda i: greet(at_z(far_first(i))))
    loop(1, 8, lambda k: greet(at_s(k)))
    for copy in local[6:]:
        copy.start()
    for copy in local[:6]:
        copy.wait()
    small[q] = jnp.concatenate(
        [
            wb_own[...],
            jnp.broadcast_to(cb_own[0:1, 0:1], (1, 128)),
            jnp.broadcast_to(cb_own[0:1, 1:2], (1, 128)),
            jnp.zeros((4, 128), F32),
        ],
        axis=0,
    )
    pl.semaphore_wait(barrier, 25)

    loop(1, 4, lambda k: send(small.at[q], small.at[q], LEFT_SMALL, SMALL, (r, lax.rem(q + k, 4))))
    send(wp.at[q], wp.at[q], LEFT_W, W_X, other_x)
    send(wp.at[q], wp.at[q], LEFT_W, W_CORE, other_core)

    own_normed = jnp.concatenate(
        [normalize(pair[q, pl.ds(t, 128, stride=4), :], ln_gain[0:1], ln_shift[0:1]) for t in range(4)], axis=0
    )

    arrived(small.at[0:3], SMALL)
    piece = dot(small[...].reshape(32, 128), own_normed, ((1,), (1,)), highest)
    for t in range(4):
        for h in range(4):
            plane0[8, y, xh, 4 * t + h : 4 * t + h + 1, :] = piece[8 * h : 8 * h + 1, 128 * t : 128 * t + 128]

    first, second = pl.ds(0, 8), pl.ds(8, 8)
    planes = (plane0, plane1)

    def quarter(i):
        j = (i + 1) // 2
        return 2 + j * (1 - 2 * lax.rem(i, 2))

    def gather_z(layer, half, lines):
        def start(i):
            place = quarter(i // 4) * 4 + lax.rem(i, 4)
            send(
                planes[layer].at[8, y, xh, lines], planes[layer].at[place, y, xh, lines],
                LEFT_Z[layer], PLANE_Z[layer] + 4 * half + i // 4, at_z(lax.rem(24 - place, 16)),
            )
        loop(1, 16, start)

    def gather_z_wait(layer, half, lines, i):
        slot = PLANE_Z[layer] + 4 * half + i

        @pl.when(i == 0)
        def _():
            arrived(planes[layer].at[9:12, y, xh, lines], slot)

        @pl.when(i > 0)
        def _():
            arrived(planes[layer].at[pl.ds(quarter(i) * 4, 4), y, xh, lines], slot)

    def around(i):
        return pl.ds(quarter(i) * 4, 4)

    def start_yx(layer, i):
        ref = planes[layer].at[around(i), y, xh, first]
        loop(1, 4, lambda k: send(ref, ref, LEFT_YX[layer], Y_FIRST[layer] + i, at_y(k)))

    def start_xy(layer, i):
        ref = planes[layer].at[around(i), y, xh, second]
        send(ref, ref, LEFT_YX[layer], X_FIRST[layer] + i, at_x)

    def next_yx(layer, i):
        arrived(planes[layer].at[around(i), 0:3, xh, first], Y_FIRST[layer] + i)
        ref = planes[layer].at[around(i), :, xh, first]
        send(ref, ref, LEFT_YX[layer], X_SECOND[layer] + i, at_x)

    def next_xy(layer, i):
        arrived(planes[layer].at[around(i), y, xh, second], X_FIRST[layer] + i)
        ref = planes[layer].at[around(i), y, :, second]
        loop(1, 4, lambda k: send(ref, ref, LEFT_YX[layer], Y_SECOND[layer] + i, at_y(k)))

    def finish(layer):
        def wait(i):
            arrived(planes[layer].at[around(i), 0:3, :, second], Y_SECOND[layer] + i)
            arrived(planes[layer].at[around(i), :, xh, first], X_SECOND[layer] + i)
        loop(0, 4, wait)

    both = pl.ds(0, 16)
    gather_z(0, 0, both)

    arrived(wp.at[q_x], W_X)
    send(wp.at[q_x], wp.at[q_x], LEFT_W, W_FWD, other_core)

    for copy in local[6:]:
        copy.wait()
    token = lax.broadcasted_iota(jnp.int32, (8, 512), 1)
    line = lax.broadcasted_iota(jnp.int32, (8, 512), 0)
    value = jnp.where(line < 4, chain[...].astype(F32), mask[...].astype(F32))
    value = jnp.where(lax.rem(token, 4) == lax.rem(line, 4), value, 0.0)
    place = lax.broadcasted_iota(jnp.int32, (512, 128), 0) // 4 == lax.broadcasted_iota(jnp.int32, (512, 128), 1)
    marks[...] = dot(value, place.astype(F32), ((1,), (0,)), highest)

    arrived(wp.at[q_core], W_CORE)
    arrived(wp.at[q_far], W_FWD)

    def weights(layer):
        for h in range(4):
            turned = wp[h, layer].T
            for ref, rows in ((wkv, turned[32:96]), (wqg, jnp.concatenate([turned[0:32], turned[96:128]], axis=0))):
                high, low = split(rows)
                ref[pl.ds(64 * h, 64), :] = jnp.concatenate([high, low], axis=1)

    def multiply(weight, features):
        high, low = split(features)
        doubled = jnp.concatenate([high, high], axis=1)
        return dot(weight[...], doubled, ((1,), (1,))) + dot(weight[:, 0:128], low, ((1,), (1,)))

    def project(a, layer):
        gain, shift = ln_gain[layer : layer + 1], ln_shift[layer : layer + 1]
        keyed = multiply(wkv, jnp.concatenate([normalize(xp[a, t], gain, shift) for t in range(4)], axis=0))
        asked = multiply(wqg, normalize(xp[a, q], gain, shift))
        for h in range(4):
            key_high, key_low = split(keyed[64 * h : 64 * h + 32])
            k3[a, h] = jnp.concatenate([key_high, key_high, key_low], axis=0)
            value_high, value_low = split(keyed[64 * h + 32 : 64 * h + 64])
            vb[a, h] = jnp.concatenate([value_high, value_low, jnp.ones((16, 512), BF16)], axis=0)
            query_high, query_low = split(asked[64 * h : 64 * h + 32] * (1.0 / math.sqrt(32)))
            q3[a, h] = jnp.concatenate([query_high, query_low, query_high], axis=0)
            gates[a, pl.ds(32 * h, 32), :] = jax.nn.sigmoid(asked[64 * h + 32 : 64 * h + 64])

    def make_bias(layer):
        chain_q = jnp.broadcast_to(marks[pl.ds(q, 1), :], (128, 128)).T
        flat = planes[layer].reshape(16, 128, 128)
        for t in range(4):
            same = (chain_q == marks[t : t + 1, :]).astype(F32)
            key_bias = (marks[4 + t : 5 + t, :] - 1.0) * 1000000000.0
            for h in range(4):
                tile = jnp.concatenate(
                    [flat[lax.rem(zz + 24 - z, 16), pl.ds(4 * t + h, 8, stride=16), :] for zz in range(16)], axis=0
                )
                if layer == 1:
                    tile = tile.T
                bias[h, :, 128 * t : 128 * t + 128] = tile + small[h, 2 + layer : 3 + layer, :] * same + key_bias

    def attend(a, layer):
        heads = []
        for h in range(4):
            score = dot(q3[a, h], k3[a, h], ((0,), (0,))) + bias[h]
            weight = jnp.exp(score - jnp.max(score, axis=-1, keepdims=True))
            weight_high, weight_low = split(weight)
            total = dot(vb[a, h], weight_high, ((1,), (1,))) + dot(vb[a, h], weight_low, ((1,), (1,)))
            heads.append((total[0:32] + total[32:64]) / total[64:65] * gates[a, pl.ds(32 * h, 32), :])
        joined = jnp.concatenate(heads, axis=0)
        return xp[a, q] + dot(joined, w_out[layer], ((0,), (0,)), highest)

    weights(0)

    def first_project(a):
        gather_z_wait(0, 0, both, a)
        start_yx(0, a)
        start_xy(0, a)
        for t in range(4):
            xp[a, t] = pair[a, pl.ds(t, 128, stride=4), :]
        project(a, 0)

        @pl.when(a > 0)
        def _():
            next_xy(0, a - 1)
            next_yx(0, a - 1)

    loop(0, 4, first_project)
    next_xy(0, 3)
    next_yx(0, 3)
    finish(0)
    make_bias(0)

    def first_attend(a):
        row = attend(a, 0)
        after[a] = row

        def leave_z(i):
            k = far_first(i)
            rows = pl.ds(pl.multiple_of(lax.rem(z + k, 16) * 8, 8), 8)
            send(after.at[a, rows], mid.at[a, z], LEFT_PAIR_Z, PAIR_Z + a, at_z(k))

        loop(0, 15, leave_z)
        mid[a, z] = after[a, pl.ds(pl.multiple_of(z * 8, 8), 8), :]
        normed = normalize(row, ln_gain[1:2], ln_shift[1:2])
        mine = dot(small[...].reshape(32, 128), normed, ((1,), (1,)), highest)
        for h in range(4):
            plane1[8, y, xh, pl.ds(4 * a + h, 1), :] = mine[8 * h + 1 : 8 * h + 2, :]

    loop(0, 2, first_attend)
    gather_z(1, 0, first)
    loop(2, 4, first_attend)
    gather_z(1, 1, second)
    weights(1)

    def over_slab(a):
        arrived(mid.at[a, 0:15], PAIR_Z + a)
        flat = mid.at[a].reshape(128, 128)
        for there in range(8):
            mid2[a, there] = flat[pl.ds(there, 16, stride=8), :]

        def leave_s(k):
            send(mid2.at[a, lax.rem(s + k, 8)], cols.at[q, s, a], LEFT_PAIR_S, PAIR_S + a, at_s(k))

        loop(1, 8, leave_s)
        cols[q, s, a] = mid2[a, s]

    def share(a):
        arrived(cols.at[q, 0:7, a], PAIR_S + a)
        block = cols.at[q, :, a]
        send(block, block, LEFT_COL, COL_X + a, other_x)
        send(block, block, LEFT_COL, COL_CORE + a, other_core)

    def pass_on(a):
        block = cols.at[q_x, :, a]
        arrived(block, COL_X + a)
        send(block, block, LEFT_COL, COL_FWD + a, other_core)

    def half_first(i):
        gather_z_wait(1, 0, first, i)
        start_yx(1, i)

    def half_second(i):
        gather_z_wait(1, 1, second, i)
        start_xy(1, i)

    def second_project(c):
        flat = cols.at[c].reshape(512, 128)
        for a in range(4):
            xp[c, a] = jnp.concatenate([flat[pl.ds(16 * a + zz, 8, stride=64), :] for zz in range(16)], axis=0)
        project(c, 1)

    over_slab(0)
    over_slab(1)
    share(0)
    loop(0, 4, half_first)
    over_slab(2)
    share(1)
    pass_on(0)
    loop(0, 4, lambda i: next_yx(1, i))
    over_slab(3)
    share(2)
    pass_on(1)
    loop(0, 4, half_second)
    share(3)
    pass_on(2)
    loop(0, 4, lambda i: next_xy(1, i))

    def own_column(i):
        @pl.when(i == 1)
        def _():
            pass_on(3)
            loop(0, 4, lambda a: arrived(cols.at[q_core, :, a], COL_CORE + a))

        @pl.when(i == 3)
        def _():
            loop(0, 4, lambda a: arrived(cols.at[q_far, :, a], COL_FWD + a))

        second_project(jnp.where(i == 0, q, jnp.where(i == 1, q_x, jnp.where(i == 2, q_core, q_far))))

    loop(0, 4, own_column)

    finish(1)
    make_bias(1)

    def out_pass_on(c):
        block = outs.at[c, q_x]
        arrived(block, OUT_X + c)
        send(block, block, LEFT_OUT, OUT_FWD + c, other_core)
        out[pl.ds(4 * q_x + c, 128, stride=16), :] = outs[c, q_x]
        arrived(outs.at[c, q_core], OUT_CORE + c)
        out[pl.ds(4 * q_core + c, 128, stride=16), :] = outs[c, q_core]

    def second_attend(c):
        result = attend(c, 1)
        outs[c, q] = result
        block = outs.at[c, q]
        send(block, block, LEFT_OUT, OUT_X + c, other_x)
        send(block, block, LEFT_OUT, OUT_CORE + c, other_core)
        out[pl.ds(4 * q + c, 128, stride=16), :] = result

        @pl.when(c > 1)
        def _():
            out_pass_on(c - 2)

    loop(0, 4, second_attend)
    loop(2, 4, out_pass_on)

    def out_end(c):
        arrived(outs.at[c, q_far], OUT_FWD + c)
        out[pl.ds(4 * q_far + c, 128, stride=16), :] = outs[c, q_far]

    loop(0, 4, out_end)

    left(small.at[0:3], LEFT_SMALL)
    left(wp.at[0:3], LEFT_W)
    for layer in range(2):
        left(planes[layer].at[0:15, 0, 0], LEFT_Z[layer])
        left(planes[layer].at[0:14], LEFT_YX[layer])
    left(mid.at[:, 0:15], LEFT_PAIR_Z)
    left(mid2.at[:, 0:7], LEFT_PAIR_S)
    left(cols.at[0:3], LEFT_COL)
    left(outs.at[0:3], LEFT_OUT)


def shards(pair_rep, residue_mask, chain_ids, ln_gain, ln_shift, w_proj, w_bias, chain_bias, w_out):
    vmem = pl.BlockSpec(memory_space=pltpu.VMEM)
    hbm = pl.BlockSpec(memory_space=pltpu.HBM)
    result = pl.pallas_call(
        kernel,
        out_shape=jax.ShapeDtypeStruct((2048, 128), F32),
        in_specs=[hbm] * 9,
        out_specs=vmem,
        scratch_shapes=[
            pltpu.VMEM((4, 512, 128), F32),
            pltpu.VMEM((1, 512), jnp.int32),
            pltpu.VMEM((1, 512), jnp.int32),
            pltpu.VMEM((2, 128), F32),
            pltpu.VMEM((2, 128), F32),
            pltpu.VMEM((2, 128), F32),
            pltpu.VMEM((1, 2), F32),
            pltpu.VMEM((2, 128, 128), F32),
            pltpu.VMEM((4, 4, 128, 128), F32),
            pltpu.VMEM((4, 2, 128, 128), F32),
            pltpu.VMEM((4, 8, 128), F32),
            pltpu.VMEM((16, 4, 2, 16, 128), F32),
            pltpu.VMEM((16, 4, 2, 16, 128), F32),
            pltpu.VMEM((4, 128, 128), F32),
            pltpu.VMEM((4, 16, 8, 128), F32),
            pltpu.VMEM((4, 8, 16, 128), F32),
            pltpu.VMEM((4, 8, 4, 16, 128), F32),
            pltpu.VMEM((4, 4, 96, 512), BF16),
            pltpu.VMEM((4, 4, 96, 128), BF16),
            pltpu.VMEM((4, 4, 80, 512), BF16),
            pltpu.VMEM((4, 128, 128), F32),
            pltpu.VMEM((4, 128, 512), F32),
            pltpu.VMEM((256, 256), BF16),
            pltpu.VMEM((256, 256), BF16),
            pltpu.VMEM((8, 128), F32),
            pltpu.VMEM((4, 4, 128, 128), F32),
            pltpu.SemaphoreType.DMA((leave.count,)),
            pltpu.SemaphoreType.DMA((arrive.count,)),
        ],
        compiler_params=pltpu.CompilerParams(
            collective_id=0, has_side_effects=True, vmem_limit_bytes=40 * 1024 * 1024
        ),
    )(
        *(
            pltpu.with_memory_space_constraint(operand, pltpu.HBM)
            for operand in (
                pair_rep,
                residue_mask.reshape(1, 512),
                chain_ids.reshape(1, 512),
                ln_gain,
                ln_shift,
                w_proj.reshape(2, 128, 128),
                w_bias.reshape(2, 128),
                chain_bias.reshape(1, 2),
                w_out,
            )
        )
    )
    return result.reshape(512, 4, 128)


def solution(mesh):
    in_specs = (
        P("row", None, None),
        P(),
        P(),
        P(),
        P(),
        P(None, None, "head", None),
        P(None, None, "head"),
        P(None, "head"),
        P(),
    )
    return jax.shard_map(shards, mesh=mesh, in_specs=in_specs, out_specs=P(None, "row", None), check_vma=False)
```

```python
import functools
import math

import jax
import jax.numpy as jnp
from jax import lax
from jax.experimental import pallas as pl
from jax.experimental.pallas import tpu as pltpu
from jax.sharding import PartitionSpec as P

highest = lax.Precision.HIGHEST
MESH = pl.DeviceIdType.MESH
F32, BF16 = jnp.float32, jnp.bfloat16

class Slots:
    def __init__(self):
        self.count = 0

    def take(self, number):
        self.count += number
        return self.count - number


arrive = Slots()
PLANE_Z = (arrive.take(4), arrive.take(8))
Y_FIRST, X_FIRST, Y_SECOND, X_SECOND = ([arrive.take(4) for _ in range(2)] for _ in range(4))
PAIR_Z, PAIR_S = arrive.take(4), arrive.take(4)
COL_CORE, COL_X, COL_FWD = arrive.take(4), arrive.take(4), arrive.take(4)
OUT_CORE, OUT_X, OUT_FWD = arrive.take(4), arrive.take(4), arrive.take(4)
SMALL, W_CORE, W_X, W_FWD = arrive.take(1), arrive.take(1), arrive.take(1), arrive.take(1)
LOCAL = OUT_CORE
leave = Slots()
LEFT_Z = (leave.take(1), leave.take(1))
LEFT_YX = (leave.take(1), leave.take(1))
LEFT_PAIR_Z, LEFT_PAIR_S, LEFT_COL, LEFT_OUT, LEFT_W, LEFT_SMALL = (leave.take(1) for _ in range(6))


def dot(a, b, dims, precision=None):
    return lax.dot_general(a, b, (dims, ((), ())), precision=precision, preferred_element_type=F32)


def split(x):
    high = x.astype(BF16)
    return high, (x - high.astype(F32)).astype(BF16)


def normalize(x, gain, shift):
    centred = x - jnp.mean(x, axis=-1, keepdims=True)
    spread = jnp.mean(centred * centred, axis=-1, keepdims=True)
    return centred * lax.rsqrt(spread + 1e-05) * gain + shift


def kernel(
    pair_in, mask_in, chain_in, gain_in, shift_in, w_own, wb_in, cb_in, w_out_in, out,
    pair, mask, chain, ln_gain, ln_shift, wb_own, cb_own, w_out,
    xp, wp, small, plane0, plane1, after, mid, mid2, cols, k3, q3, vb, gates, bias, wkv, wqg, w_out3, marks, outs, ss, rs,
):
    r, head = lax.axis_index("row"), lax.axis_index("head")
    z, s = r // 8, lax.rem(r, 8)
    y, xh = s // 2, lax.rem(s, 2)
    core, xlo = lax.rem(head, 2), head // 2
    other_core = (r, xlo * 2 + 1 - core)
    other_x = (r, (1 - xlo) * 2 + core)
    head_core, head_x, head_far = other_core[1], other_x[1], (1 - xlo) * 2 + 1 - core
    side = lax.rem(xlo + xh, 2)
    q, q_core = side * 2 + core, side * 2 + 1 - core
    q_x, q_far = (1 - side) * 2 + core, (1 - side) * 2 + 1 - core

    def twin(there):
        other = lax.rem(lax.rem(there, 2) + xh, 2)
        return (z * 8 + there, lax.rem(xlo + other, 2) * 2 + core)

    def at_z(k):
        return (lax.rem(z + k, 16) * 8 + s, head)

    def at_y(k):
        return (z * 8 + lax.rem(y + k, 4) * 2 + xh, head)

    def at_s(k):
        return twin(lax.rem(s + k, 8))

    at_x = twin(y * 2 + 1 - xh)

    def send(src, dst, left, slot, device):
        pltpu.make_async_remote_copy(
            src_ref=src, dst_ref=dst, send_sem=ss.at[left], recv_sem=rs.at[slot],
            device_id=device, device_id_type=MESH,
        ).start()

    def arrived(ref, slot):
        pltpu.make_async_remote_copy(
            src_ref=ref, dst_ref=ref, send_sem=ss.at[0], recv_sem=rs.at[slot],
            device_id=at_x, device_id_type=MESH,
        ).wait_recv()

    def left(ref, slot):
        pltpu.make_async_remote_copy(
            src_ref=ref, dst_ref=ref, send_sem=ss.at[slot], recv_sem=rs.at[0],
            device_id=at_x, device_id_type=MESH,
        ).wait_send()

    def loop(low, high, body):
        def step(i, carry):
            body(i)
            return carry
        lax.fori_loop(low, high, step, 0)

    def far_first(i):
        j = (i + 1) // 2
        return 8 + j * (2 * lax.rem(i, 2) - 1)

    local = [
        pltpu.make_async_copy(pair_in.at[q], pair.at[q], rs.at[LOCAL]),
        pltpu.make_async_copy(gain_in, ln_gain, rs.at[LOCAL + 1]),
        pltpu.make_async_copy(shift_in, ln_shift, rs.at[LOCAL + 2]),
        pltpu.make_async_copy(wb_in, wb_own, rs.at[LOCAL + 3]),
        pltpu.make_async_copy(cb_in, cb_own, rs.at[LOCAL + 4]),
        pltpu.make_async_copy(w_own, wp.at[head], rs.at[LOCAL + 5]),
        pltpu.make_async_copy(mask_in, mask, rs.at[LOCAL + 6]),
        pltpu.make_async_copy(chain_in, chain, rs.at[LOCAL + 7]),
        pltpu.make_async_copy(w_out_in, w_out, rs.at[LOCAL + 8]),
    ] + [
        pltpu.make_async_copy(
            pair_in.at[lax.rem(q + k, 4)], pair.at[lax.rem(q + k, 4)], rs.at[LOCAL + 8 + k]
        )
        for k in range(1, 4)
    ]
    for copy in local[:6]:
        copy.start()

    barrier = pltpu.get_barrier_semaphore()

    def greet(device):
        pl.semaphore_signal(barrier, inc=1, device_id=device, device_id_type=MESH)

    loop(1, 4, lambda k: greet((r, lax.rem(head + k, 4))))
    loop(0, 15, lambda i: greet(at_z(far_first(i))))
    loop(1, 8, lambda k: greet(at_s(k)))
    for copy in local[6:]:
        copy.start()
    for copy in local[:6]:
        copy.wait()
    small[head] = jnp.concatenate(
        [
            wb_own[...],
            jnp.broadcast_to(cb_own[0:1, 0:1], (1, 128)),
            jnp.broadcast_to(cb_own[0:1, 1:2], (1, 128)),
            jnp.zeros((4, 128), F32),
        ],
        axis=0,
    )
    pl.semaphore_wait(barrier, 25)

    loop(1, 4, lambda k: send(small.at[head], small.at[head], LEFT_SMALL, SMALL, (r, lax.rem(head + k, 4))))
    send(wp.at[head], wp.at[head], LEFT_W, W_X, other_x)
    send(wp.at[head], wp.at[head], LEFT_W, W_CORE, other_core)

    own_normed = jnp.concatenate(
        [normalize(pair[q, pl.ds(t, 128, stride=4), :], ln_gain[0:1], ln_shift[0:1]) for t in range(4)], axis=0
    )

    arrived(small.at[0:3], SMALL)
    piece = dot(small[...].reshape(32, 128), own_normed, ((1,), (1,)), highest)
    for t in range(4):
        for h in range(4):
            plane0[8, y, xh, 4 * t + h : 4 * t + h + 1, :] = piece[8 * h : 8 * h + 1, 128 * t : 128 * t + 128]

    first, second = pl.ds(0, 8), pl.ds(8, 8)
    planes = (plane0, plane1)

    def quarter(i):
        j = (i + 1) // 2
        return 2 + j * (1 - 2 * lax.rem(i, 2))

    def gather_z(layer, half, lines):
        def start(i):
            place = quarter(i // 4) * 4 + lax.rem(i, 4)
            send(
                planes[layer].at[8, y, xh, lines], planes[layer].at[place, y, xh, lines],
                LEFT_Z[layer], PLANE_Z[layer] + 4 * half + i // 4, at_z(lax.rem(24 - place, 16)),
            )
        loop(1, 16, start)

    def gather_z_wait(layer, half, lines, i):
        slot = PLANE_Z[layer] + 4 * half + i

        @pl.when(i == 0)
        def _():
            arrived(planes[layer].at[9:12, y, xh, lines], slot)

        @pl.when(i > 0)
        def _():
            arrived(planes[layer].at[pl.ds(quarter(i) * 4, 4), y, xh, lines], slot)

    def around(i):
        return pl.ds(quarter(i) * 4, 4)

    def start_yx(layer, i):
        ref = planes[layer].at[around(i), y, xh, first]
        loop(1, 4, lambda k: send(ref, ref, LEFT_YX[layer], Y_FIRST[layer] + i, at_y(k)))

    def start_xy(layer, i):
        ref = planes[layer].at[around(i), y, xh, second]
        send(ref, ref, LEFT_YX[layer], X_FIRST[layer] + i, at_x)

    def next_yx(layer, i):
        arrived(planes[layer].at[around(i), 0:3, xh, first], Y_FIRST[layer] + i)
        ref = planes[layer].at[around(i), :, xh, first]
        send(ref, ref, LEFT_YX[layer], X_SECOND[layer] + i, at_x)

    def next_xy(layer, i):
        arrived(planes[layer].at[around(i), y, xh, second], X_FIRST[layer] + i)
        ref = planes[layer].at[around(i), y, :, second]
        loop(1, 4, lambda k: send(ref, ref, LEFT_YX[layer], Y_SECOND[layer] + i, at_y(k)))

    def finish(layer):
        def wait(i):
            arrived(planes[layer].at[around(i), 0:3, :, second], Y_SECOND[layer] + i)
            arrived(planes[layer].at[around(i), :, xh, first], X_SECOND[layer] + i)
        loop(0, 4, wait)

    both = pl.ds(0, 16)
    gather_z(0, 0, both)

    arrived(wp.at[head_x], W_X)
    send(wp.at[head_x], wp.at[head_x], LEFT_W, W_FWD, other_core)

    for copy in local[6:]:
        copy.wait()
    token = lax.broadcasted_iota(jnp.int32, (8, 512), 1)
    line = lax.broadcasted_iota(jnp.int32, (8, 512), 0)
    value = jnp.where(line < 4, chain[...].astype(F32), mask[...].astype(F32))
    value = jnp.where(lax.rem(token, 4) == lax.rem(line, 4), value, 0.0)
    place = lax.broadcasted_iota(jnp.int32, (512, 128), 0) // 4 == lax.broadcasted_iota(jnp.int32, (512, 128), 1)
    marks[...] = dot(value, place.astype(F32), ((1,), (0,)), highest)

    arrived(wp.at[head_core], W_CORE)
    arrived(wp.at[head_far], W_FWD)

    def weights(layer):
        out_high, out_low = split(w_out[layer])
        w_out3[layer] = jnp.concatenate([out_high, out_high, out_low], axis=0)
        for h in range(4):
            turned = wp[h, layer].T
            for ref, rows in ((wkv, turned[32:96]), (wqg, jnp.concatenate([turned[0:32], turned[96:128]], axis=0))):
                high, low = split(rows)
                ref[pl.ds(64 * h, 64), :] = jnp.concatenate([high, low], axis=1)

    def multiply(weight, features):
        high, low = split(features)
        doubled = jnp.concatenate([high, high], axis=1)
        return dot(weight[...], doubled, ((1,), (1,))) + dot(weight[:, 0:128], low, ((1,), (1,)))

    def project(a, layer):
        gain, shift = ln_gain[layer : layer + 1], ln_shift[layer : layer + 1]
        keyed = multiply(wkv, jnp.concatenate([normalize(xp[a, t], gain, shift) for t in range(4)], axis=0))
        asked = multiply(wqg, normalize(xp[a, q], gain, shift))
        for h in range(4):
            key_high, key_low = split(keyed[64 * h : 64 * h + 32])
            k3[a, h] = jnp.concatenate([key_high, key_high, key_low], axis=0)
            value_high, value_low = split(keyed[64 * h + 32 : 64 * h + 64])
            vb[a, h] = jnp.concatenate([value_high, value_low, jnp.ones((16, 512), BF16)], axis=0)
            query_high, query_low = split(asked[64 * h : 64 * h + 32] * (1.0 / math.sqrt(32)))
            q3[a, h] = jnp.concatenate([query_high, query_low, query_high], axis=0)
            gates[a, pl.ds(32 * h, 32), :] = jax.nn.sigmoid(asked[64 * h + 32 : 64 * h + 64])

    def make_bias(layer):
        chain_q = jnp.broadcast_to(marks[pl.ds(q, 1), :], (128, 128)).T
        flat = planes[layer].reshape(16, 128, 128)
        for t in range(4):
            same = (chain_q == marks[t : t + 1, :]).astype(F32)
            key_bias = (marks[4 + t : 5 + t, :] - 1.0) * 1000000000.0
            for h in range(4):
                tile = jnp.concatenate(
                    [flat[lax.rem(zz + 24 - z, 16), pl.ds(4 * t + h, 8, stride=16), :] for zz in range(16)], axis=0
                )
                if layer == 1:
                    tile = tile.T
                bias[h, :, 128 * t : 128 * t + 128] = tile + small[h, 2 + layer : 3 + layer, :] * same + key_bias

    def attend(a, layer):
        four = range(4)
        scores = [dot(q3[a, h], k3[a, h], ((0,), (0,))) + bias[h] for h in four]
        tops = [jnp.max(scores[h], axis=-1, keepdims=True) for h in four]
        weights = [split(jnp.exp(scores[h] - tops[h])) for h in four]
        totals = [
            (dot(weights[h][0], vb[a, h], ((1,), (1,))) + dot(weights[h][1], vb[a, h], ((1,), (1,)))).T for h in four
        ]
        heads = [
            (totals[h][0:32] + totals[h][32:64]) / totals[h][64:65] * gates[a, pl.ds(32 * h, 32), :] for h in four
        ]
        high, low = split(jnp.concatenate(heads, axis=0))
        return xp[a, q] + dot(jnp.concatenate([high, low, high], axis=0), w_out3[layer], ((0,), (0,)))

    weights(0)

    def first_project(a):
        gather_z_wait(0, 0, both, a)
        start_yx(0, a)
        start_xy(0, a)
        for t in range(4):
            xp[a, t] = pair[a, pl.ds(t, 128, stride=4), :]
        project(a, 0)

        @pl.when(a > 0)
        def _():
            next_xy(0, a - 1)
            next_yx(0, a - 1)

    loop(0, 4, first_project)
    next_xy(0, 3)
    next_yx(0, 3)
    finish(0)
    make_bias(0)

    def first_attend(a):
        row = attend(a, 0)
        after[a] = row

        def leave_z(i):
            k = far_first(i)
            rows = pl.ds(pl.multiple_of(lax.rem(z + k, 16) * 8, 8), 8)
            send(after.at[a, rows], mid.at[a, z], LEFT_PAIR_Z, PAIR_Z + a, at_z(k))

        loop(0, 15, leave_z)
        mid[a, z] = after[a, pl.ds(pl.multiple_of(z * 8, 8), 8), :]
        normed = normalize(row, ln_gain[1:2], ln_shift[1:2])
        mine = dot(small[...].reshape(32, 128), normed, ((1,), (1,)), highest)
        for h in range(4):
            plane1[8, y, xh, pl.ds(4 * a + h, 1), :] = mine[8 * h + 1 : 8 * h + 2, :]

    loop(0, 2, first_attend)
    gather_z(1, 0, first)
    loop(2, 4, first_attend)
    gather_z(1, 1, second)
    weights(1)

    def over_slab(a):
        arrived(mid.at[a, 0:15], PAIR_Z + a)
        flat = mid.at[a].reshape(128, 128)
        for there in range(8):
            mid2[a, there] = flat[pl.ds(there, 16, stride=8), :]

        def leave_s(k):
            send(mid2.at[a, lax.rem(s + k, 8)], cols.at[q, s, a], LEFT_PAIR_S, PAIR_S + a, at_s(k))

        loop(1, 8, leave_s)
        cols[q, s, a] = mid2[a, s]

    def share(a):
        arrived(cols.at[q, 0:7, a], PAIR_S + a)
        block = cols.at[q, :, a]
        send(block, block, LEFT_COL, COL_X + a, other_x)
        send(block, block, LEFT_COL, COL_CORE + a, other_core)

    def pass_on(a):
        block = cols.at[q_x, :, a]
        arrived(block, COL_X + a)
        send(block, block, LEFT_COL, COL_FWD + a, other_core)

    def half_first(i):
        gather_z_wait(1, 0, first, i)
        start_yx(1, i)

    def half_second(i):
        gather_z_wait(1, 1, second, i)
        start_xy(1, i)

    def second_project(c):
        flat = cols.at[c].reshape(512, 128)
        for a in range(4):
            xp[c, a] = jnp.concatenate([flat[pl.ds(16 * a + zz, 8, stride=64), :] for zz in range(16)], axis=0)
        project(c, 1)

    over_slab(0)
    over_slab(1)
    share(0)
    loop(0, 4, half_first)
    over_slab(2)
    share(1)
    pass_on(0)
    loop(0, 4, lambda i: next_yx(1, i))
    over_slab(3)
    share(2)
    pass_on(1)
    loop(0, 4, half_second)
    share(3)
    pass_on(2)
    loop(0, 4, lambda i: next_xy(1, i))

    def own_column(i):
        @pl.when(i == 1)
        def _():
            pass_on(3)
            loop(0, 4, lambda a: arrived(cols.at[q_core, :, a], COL_CORE + a))

        @pl.when(i == 3)
        def _():
            loop(0, 4, lambda a: arrived(cols.at[q_far, :, a], COL_FWD + a))

        second_project(jnp.where(i == 0, q, jnp.where(i == 1, q_x, jnp.where(i == 2, q_core, q_far))))

    loop(0, 4, own_column)

    finish(1)
    make_bias(1)

    def out_pass_on(c):
        block = outs.at[c, q_x]
        arrived(block, OUT_X + c)
        send(block, block, LEFT_OUT, OUT_FWD + c, other_core)
        out[pl.ds(4 * q_x + c, 128, stride=16), :] = outs[c, q_x]
        arrived(outs.at[c, q_core], OUT_CORE + c)
        out[pl.ds(4 * q_core + c, 128, stride=16), :] = outs[c, q_core]

    def second_attend(c):
        result = attend(c, 1)
        outs[c, q] = result
        block = outs.at[c, q]
        send(block, block, LEFT_OUT, OUT_X + c, other_x)
        send(block, block, LEFT_OUT, OUT_CORE + c, other_core)
        out[pl.ds(4 * q + c, 128, stride=16), :] = result

        @pl.when(c > 1)
        def _():
            out_pass_on(c - 2)

    loop(0, 4, second_attend)
    loop(2, 4, out_pass_on)

    def out_end(c):
        arrived(outs.at[c, q_far], OUT_FWD + c)
        out[pl.ds(4 * q_far + c, 128, stride=16), :] = outs[c, q_far]

    loop(0, 4, out_end)

    left(small.at[0:3], LEFT_SMALL)
    left(wp.at[0:3], LEFT_W)
    for layer in range(2):
        left(planes[layer].at[0:15, 0, 0], LEFT_Z[layer])
        left(planes[layer].at[0:14], LEFT_YX[layer])
    left(mid.at[:, 0:15], LEFT_PAIR_Z)
    left(mid2.at[:, 0:7], LEFT_PAIR_S)
    left(cols.at[0:3], LEFT_COL)
    left(outs.at[0:3], LEFT_OUT)


def shards(pair_rep, residue_mask, chain_ids, ln_gain, ln_shift, w_proj, w_bias, chain_bias, w_out):
    vmem = pl.BlockSpec(memory_space=pltpu.VMEM)
    hbm = pl.BlockSpec(memory_space=pltpu.HBM)
    result = pl.pallas_call(
        kernel,
        out_shape=jax.ShapeDtypeStruct((2048, 128), F32),
        in_specs=[hbm] * 9,
        out_specs=vmem,
        scratch_shapes=[
            pltpu.VMEM((4, 512, 128), F32),
            pltpu.VMEM((1, 512), jnp.int32),
            pltpu.VMEM((1, 512), jnp.int32),
            pltpu.VMEM((2, 128), F32),
            pltpu.VMEM((2, 128), F32),
            pltpu.VMEM((2, 128), F32),
            pltpu.VMEM((1, 2), F32),
            pltpu.VMEM((2, 128, 128), F32),
            pltpu.VMEM((4, 4, 128, 128), F32),
            pltpu.VMEM((4, 2, 128, 128), F32),
            pltpu.VMEM((4, 8, 128), F32),
            pltpu.VMEM((16, 4, 2, 16, 128), F32),
            pltpu.VMEM((16, 4, 2, 16, 128), F32),
            pltpu.VMEM((4, 128, 128), F32),
            pltpu.VMEM((4, 16, 8, 128), F32),
            pltpu.VMEM((4, 8, 16, 128), F32),
            pltpu.VMEM((4, 8, 4, 16, 128), F32),
            pltpu.VMEM((4, 4, 96, 512), BF16),
            pltpu.VMEM((4, 4, 96, 128), BF16),
            pltpu.VMEM((4, 4, 80, 512), BF16),
            pltpu.VMEM((4, 128, 128), F32),
            pltpu.VMEM((4, 128, 512), F32),
            pltpu.VMEM((256, 256), BF16),
            pltpu.VMEM((256, 256), BF16),
            pltpu.VMEM((2, 384, 128), BF16),
            pltpu.VMEM((8, 128), F32),
            pltpu.VMEM((4, 4, 128, 128), F32),
            pltpu.SemaphoreType.DMA((leave.count,)),
            pltpu.SemaphoreType.DMA((arrive.count,)),
        ],
        compiler_params=pltpu.CompilerParams(
            collective_id=0, has_side_effects=True, vmem_limit_bytes=40 * 1024 * 1024
        ),
    )(
        *(
            pltpu.with_memory_space_constraint(operand, pltpu.HBM)
            for operand in (
                pair_rep,
                residue_mask.reshape(1, 512),
                chain_ids.reshape(1, 512),
                ln_gain,
                ln_shift,
                w_proj.reshape(2, 128, 128),
                w_bias.reshape(2, 128),
                chain_bias.reshape(1, 2),
                w_out,
            )
        )
    )
    return result.reshape(512, 4, 128)


def solution(mesh):
    in_specs = (
        P("row", None, None),
        P(),
        P(),
        P(),
        P(),
        P(None, None, "head", None),
        P(None, None, "head"),
        P(None, "head"),
        P(),
    )
    return jax.shard_map(shards, mesh=mesh, in_specs=in_specs, out_specs=P(None, "row", None), check_vma=False)
```

```python
import functools
import math

import jax
import jax.numpy as jnp
from jax import lax
from jax.experimental import pallas as pl
from jax.experimental.pallas import tpu as pltpu
from jax.sharding import PartitionSpec as P

highest = lax.Precision.HIGHEST
MESH = pl.DeviceIdType.MESH
F32, BF16 = jnp.float32, jnp.bfloat16

class Slots:
    def __init__(self):
        self.count = 0

    def take(self, number):
        self.count += number
        return self.count - number


arrive = Slots()
PLANE_Z = (arrive.take(4), arrive.take(8))
Y_FIRST, X_FIRST, Y_SECOND, X_SECOND = ([arrive.take(4) for _ in range(2)] for _ in range(4))
PAIR_Z, PAIR_S = arrive.take(4), arrive.take(4)
COL_CORE, COL_X, COL_FWD = arrive.take(4), arrive.take(4), arrive.take(4)
OUT_CORE, OUT_X, OUT_FWD = arrive.take(4), arrive.take(4), arrive.take(4)
SMALL, W_CORE, W_X, W_FWD = arrive.take(1), arrive.take(1), arrive.take(1), arrive.take(1)
LOCAL = OUT_CORE
leave = Slots()
LEFT_Z = (leave.take(1), leave.take(1))
LEFT_YX = (leave.take(1), leave.take(1))
LEFT_PAIR_Z, LEFT_PAIR_S, LEFT_COL, LEFT_OUT, LEFT_W, LEFT_SMALL = (leave.take(1) for _ in range(6))


def dot(a, b, dims, precision=None):
    return lax.dot_general(a, b, (dims, ((), ())), precision=precision, preferred_element_type=F32)


def split(x):
    high = x.astype(BF16)
    return high, (x - high.astype(F32)).astype(BF16)


def normalize(x, gain, shift):
    centred = x - jnp.mean(x, axis=-1, keepdims=True)
    spread = jnp.mean(centred * centred, axis=-1, keepdims=True)
    return centred * lax.rsqrt(spread + 1e-05) * gain + shift


def kernel(
    pair_in, mask_in, chain_in, gain_in, shift_in, w_own, wb_in, cb_in, w_out_in, out,
    pair, mask, chain, ln_gain, ln_shift, wb_own, cb_own, w_out,
    xp, wp, small, plane0, plane1, after, mid, mid2, cols, k3, q3, vb, gates, bias, wkv, wqg, w_out3, marks, outs, ss, rs,
):
    r, head = lax.axis_index("row"), lax.axis_index("head")
    z, s = r // 8, lax.rem(r, 8)
    y, xh = s // 2, lax.rem(s, 2)
    core, xlo = lax.rem(head, 2), head // 2
    other_core = (r, xlo * 2 + 1 - core)
    other_x = (r, (1 - xlo) * 2 + core)
    head_core, head_x, head_far = other_core[1], other_x[1], (1 - xlo) * 2 + 1 - core
    side = lax.rem(xlo + xh, 2)
    q, q_core = side * 2 + core, side * 2 + 1 - core
    q_x, q_far = (1 - side) * 2 + core, (1 - side) * 2 + 1 - core

    def twin(there):
        other = lax.rem(lax.rem(there, 2) + xh, 2)
        return (z * 8 + there, lax.rem(xlo + other, 2) * 2 + core)

    def at_z(k):
        return (lax.rem(z + k, 16) * 8 + s, head)

    def at_y(k):
        return (z * 8 + lax.rem(y + k, 4) * 2 + xh, head)

    def at_s(k):
        return twin(lax.rem(s + k, 8))

    at_x = twin(y * 2 + 1 - xh)

    def send(src, dst, left, slot, device):
        pltpu.make_async_remote_copy(
            src_ref=src, dst_ref=dst, send_sem=ss.at[left], recv_sem=rs.at[slot],
            device_id=device, device_id_type=MESH,
        ).start()

    def arrived(ref, slot):
        pltpu.make_async_remote_copy(
            src_ref=ref, dst_ref=ref, send_sem=ss.at[0], recv_sem=rs.at[slot],
            device_id=at_x, device_id_type=MESH,
        ).wait_recv()

    def left(ref, slot):
        pltpu.make_async_remote_copy(
            src_ref=ref, dst_ref=ref, send_sem=ss.at[slot], recv_sem=rs.at[0],
            device_id=at_x, device_id_type=MESH,
        ).wait_send()

    def loop(low, high, body):
        def step(i, carry):
            body(i)
            return carry
        lax.fori_loop(low, high, step, 0)

    def far_first(i):
        j = (i + 1) // 2
        return 8 + j * (2 * lax.rem(i, 2) - 1)

    local = [
        pltpu.make_async_copy(pair_in.at[q], pair.at[q], rs.at[LOCAL]),
        pltpu.make_async_copy(gain_in, ln_gain, rs.at[LOCAL + 1]),
        pltpu.make_async_copy(shift_in, ln_shift, rs.at[LOCAL + 2]),
        pltpu.make_async_copy(wb_in, wb_own, rs.at[LOCAL + 3]),
        pltpu.make_async_copy(cb_in, cb_own, rs.at[LOCAL + 4]),
        pltpu.make_async_copy(w_own, wp.at[head], rs.at[LOCAL + 5]),
        pltpu.make_async_copy(mask_in, mask, rs.at[LOCAL + 6]),
        pltpu.make_async_copy(chain_in, chain, rs.at[LOCAL + 7]),
        pltpu.make_async_copy(w_out_in, w_out, rs.at[LOCAL + 8]),
    ] + [
        pltpu.make_async_copy(
            pair_in.at[lax.rem(q + k, 4)], pair.at[lax.rem(q + k, 4)], rs.at[LOCAL + 8 + k]
        )
        for k in range(1, 4)
    ]
    for copy in local[:6]:
        copy.start()

    barrier = pltpu.get_barrier_semaphore()

    def greet(device):
        pl.semaphore_signal(barrier, inc=1, device_id=device, device_id_type=MESH)

    loop(1, 4, lambda k: greet((r, lax.rem(head + k, 4))))
    loop(0, 15, lambda i: greet(at_z(far_first(i))))
    loop(1, 8, lambda k: greet(at_s(k)))
    for copy in local[6:]:
        copy.start()
    for copy in local[:6]:
        copy.wait()
    small[head] = jnp.concatenate(
        [
            wb_own[...],
            jnp.broadcast_to(cb_own[0:1, 0:1], (1, 128)),
            jnp.broadcast_to(cb_own[0:1, 1:2], (1, 128)),
            jnp.zeros((4, 128), F32),
        ],
        axis=0,
    )
    pl.semaphore_wait(barrier, 25)

    loop(1, 4, lambda k: send(small.at[head], small.at[head], LEFT_SMALL, SMALL, (r, lax.rem(head + k, 4))))
    send(wp.at[head], wp.at[head], LEFT_W, W_X, other_x)
    send(wp.at[head], wp.at[head], LEFT_W, W_CORE, other_core)

    own_normed = jnp.concatenate(
        [normalize(pair[q, pl.ds(t, 128, stride=4), :], ln_gain[0:1], ln_shift[0:1]) for t in range(4)], axis=0
    )

    arrived(small.at[0:3], SMALL)
    piece = dot(small[...].reshape(32, 128), own_normed, ((1,), (1,)), highest)
    for t in range(4):
        for h in range(4):
            plane0[8, y, xh, 4 * t + h : 4 * t + h + 1, :] = piece[8 * h : 8 * h + 1, 128 * t : 128 * t + 128]

    first, second = pl.ds(0, 8), pl.ds(8, 8)
    planes = (plane0, plane1)

    def quarter(i):
        j = (i + 1) // 2
        return 2 + j * (1 - 2 * lax.rem(i, 2))

    def gather_z(layer, half, lines):
        def start(i):
            place = quarter(i // 4) * 4 + lax.rem(i, 4)
            send(
                planes[layer].at[8, y, xh, lines], planes[layer].at[place, y, xh, lines],
                LEFT_Z[layer], PLANE_Z[layer] + 4 * half + i // 4, at_z(lax.rem(24 - place, 16)),
            )
        loop(1, 16, start)

    def gather_z_wait(layer, half, lines, i):
        slot = PLANE_Z[layer] + 4 * half + i

        @pl.when(i == 0)
        def _():
            arrived(planes[layer].at[9:12, y, xh, lines], slot)

        @pl.when(i > 0)
        def _():
            arrived(planes[layer].at[pl.ds(quarter(i) * 4, 4), y, xh, lines], slot)

    def around(i):
        return pl.ds(quarter(i) * 4, 4)

    def start_yx(layer, i):
        ref = planes[layer].at[around(i), y, xh, first]
        loop(1, 4, lambda k: send(ref, ref, LEFT_YX[layer], Y_FIRST[layer] + i, at_y(k)))

    def start_xy(layer, i):
        ref = planes[layer].at[around(i), y, xh, second]
        send(ref, ref, LEFT_YX[layer], X_FIRST[layer] + i, at_x)

    def next_yx(layer, i):
        arrived(planes[layer].at[around(i), 0:3, xh, first], Y_FIRST[layer] + i)
        ref = planes[layer].at[around(i), :, xh, first]
        send(ref, ref, LEFT_YX[layer], X_SECOND[layer] + i, at_x)

    def next_xy(layer, i):
        arrived(planes[layer].at[around(i), y, xh, second], X_FIRST[layer] + i)
        ref = planes[layer].at[around(i), y, :, second]
        loop(1, 4, lambda k: send(ref, ref, LEFT_YX[layer], Y_SECOND[layer] + i, at_y(k)))

    def finish(layer):
        def wait(i):
            arrived(planes[layer].at[around(i), 0:3, :, second], Y_SECOND[layer] + i)
            arrived(planes[layer].at[around(i), :, xh, first], X_SECOND[layer] + i)
        loop(0, 4, wait)

    both = pl.ds(0, 16)
    gather_z(0, 0, both)

    arrived(wp.at[head_x], W_X)
    send(wp.at[head_x], wp.at[head_x], LEFT_W, W_FWD, other_core)

    for copy in local[6:]:
        copy.wait()
    token = lax.broadcasted_iota(jnp.int32, (8, 512), 1)
    line = lax.broadcasted_iota(jnp.int32, (8, 512), 0)
    value = jnp.where(line < 4, chain[...].astype(F32), mask[...].astype(F32))
    value = jnp.where(lax.rem(token, 4) == lax.rem(line, 4), value, 0.0)
    place = lax.broadcasted_iota(jnp.int32, (512, 128), 0) // 4 == lax.broadcasted_iota(jnp.int32, (512, 128), 1)
    marks[...] = dot(value, place.astype(F32), ((1,), (0,)), highest)

    gather_z_wait(0, 0, both, 0)
    start_yx(0, 0)
    start_xy(0, 0)
    arrived(wp.at[head_core], W_CORE)
    arrived(wp.at[head_far], W_FWD)

    def weights(layer):
        out_high, out_low = split(w_out[layer])
        w_out3[layer] = jnp.concatenate([out_high, out_high, out_low], axis=0)
        for h in range(4):
            turned = wp[h, layer].T
            for ref, rows in ((wkv, turned[32:96]), (wqg, jnp.concatenate([turned[0:32], turned[96:128]], axis=0))):
                high, low = split(rows)
                ref[pl.ds(64 * h, 64), :] = jnp.concatenate([high, low], axis=1)

    def multiply(weight, features):
        high, low = split(features)
        doubled = jnp.concatenate([high, high], axis=1)
        return dot(weight[...], doubled, ((1,), (1,))) + dot(weight[:, 0:128], low, ((1,), (1,)))

    def project(a, layer):
        gain, shift = ln_gain[layer : layer + 1], ln_shift[layer : layer + 1]
        keyed = multiply(wkv, jnp.concatenate([normalize(xp[a, t], gain, shift) for t in range(4)], axis=0))
        asked = multiply(wqg, normalize(xp[a, q], gain, shift))
        for h in range(4):
            key_high, key_low = split(keyed[64 * h : 64 * h + 32])
            k3[a, h] = jnp.concatenate([key_high, key_high, key_low], axis=0)
            value_high, value_low = split(keyed[64 * h + 32 : 64 * h + 64])
            vb[a, h] = jnp.concatenate([value_high, value_low, jnp.ones((16, 512), BF16)], axis=0)
            query_high, query_low = split(asked[64 * h : 64 * h + 32] * (1.0 / math.sqrt(32)))
            q3[a, h] = jnp.concatenate([query_high, query_low, query_high], axis=0)
            gates[a, pl.ds(32 * h, 32), :] = jax.nn.sigmoid(asked[64 * h + 32 : 64 * h + 64])

    def make_bias(layer):
        chain_q = jnp.broadcast_to(marks[pl.ds(q, 1), :], (128, 128)).T
        flat = planes[layer].reshape(16, 128, 128)
        for t in range(4):
            same = (chain_q == marks[t : t + 1, :]).astype(F32)
            key_bias = (marks[4 + t : 5 + t, :] - 1.0) * 1000000000.0
            for h in range(4):
                tile = jnp.concatenate(
                    [flat[lax.rem(zz + 24 - z, 16), pl.ds(4 * t + h, 8, stride=16), :] for zz in range(16)], axis=0
                )
                if layer == 1:
                    tile = tile.T
                bias[h, :, 128 * t : 128 * t + 128] = tile + small[h, 2 + layer : 3 + layer, :] * same + key_bias

    def attend(a, layer):
        four = range(4)
        scores = [dot(q3[a, h], k3[a, h], ((0,), (0,))) + bias[h] for h in four]
        tops = [jnp.max(scores[h], axis=-1, keepdims=True) for h in four]
        weights = [split(jnp.exp(scores[h] - tops[h])) for h in four]
        totals = [
            (dot(weights[h][0], vb[a, h], ((1,), (1,))) + dot(weights[h][1], vb[a, h], ((1,), (1,)))).T for h in four
        ]
        heads = [
            (totals[h][0:32] + totals[h][32:64]) / totals[h][64:65] * gates[a, pl.ds(32 * h, 32), :] for h in four
        ]
        high, low = split(jnp.concatenate(heads, axis=0))
        return xp[a, q] + dot(jnp.concatenate([high, low, high], axis=0), w_out3[layer], ((0,), (0,)))

    weights(0)

    def first_project(a):
        @pl.when(a > 0)
        def _():
            gather_z_wait(0, 0, both, a)
            start_yx(0, a)
            start_xy(0, a)

        for t in range(4):
            xp[a, t] = pair[a, pl.ds(t, 128, stride=4), :]
        project(a, 0)

        @pl.when(a > 0)
        def _():
            next_xy(0, a - 1)
            next_yx(0, a - 1)

    loop(0, 4, first_project)
    next_xy(0, 3)
    next_yx(0, 3)
    finish(0)
    make_bias(0)

    def first_attend(a):
        row = attend(a, 0)
        after[a] = row

        for k in (8, 9, 7, 10, 6, 11, 5, 12, 4, 13, 3, 14, 2, 15, 1):
            rows = pl.ds(pl.multiple_of(lax.rem(z + k, 16) * 8, 8), 8)
            send(after.at[a, rows], mid.at[a, z], LEFT_PAIR_Z, PAIR_Z + a, at_z(k))
        mid[a, z] = after[a, pl.ds(pl.multiple_of(z * 8, 8), 8), :]
        normed = normalize(row, ln_gain[1:2], ln_shift[1:2])
        mine = dot(small[...].reshape(32, 128), normed, ((1,), (1,)), highest)
        for h in range(4):
            plane1[8, y, xh, pl.ds(4 * a + h, 1), :] = mine[8 * h + 1 : 8 * h + 2, :]

    loop(0, 2, first_attend)
    gather_z(1, 0, first)
    loop(2, 4, first_attend)
    gather_z(1, 1, second)
    weights(1)

    def over_slab(a):
        arrived(mid.at[a, 0:15], PAIR_Z + a)
        flat = mid.at[a].reshape(128, 128)
        for there in range(8):
            mid2[a, there] = flat[pl.ds(there, 16, stride=8), :]

        def leave_s(k):
            send(mid2.at[a, lax.rem(s + k, 8)], cols.at[q, s, a], LEFT_PAIR_S, PAIR_S + a, at_s(k))

        loop(1, 8, leave_s)
        cols[q, s, a] = mid2[a, s]

    def share(a):
        arrived(cols.at[q, 0:7, a], PAIR_S + a)
        block = cols.at[q, :, a]
        send(block, block, LEFT_COL, COL_X + a, other_x)
        send(block, block, LEFT_COL, COL_CORE + a, other_core)

    def pass_on(a):
        block = cols.at[q_x, :, a]
        arrived(block, COL_X + a)
        send(block, block, LEFT_COL, COL_FWD + a, other_core)

    def half_first(i):
        gather_z_wait(1, 0, first, i)
        start_yx(1, i)

    def half_second(i):
        gather_z_wait(1, 1, second, i)
        start_xy(1, i)

    def second_project(c):
        flat = cols.at[c].reshape(512, 128)
        for a in range(4):
            xp[c, a] = jnp.concatenate([flat[pl.ds(16 * a + zz, 8, stride=64), :] for zz in range(16)], axis=0)
        project(c, 1)

    over_slab(0)
    over_slab(1)
    share(0)
    loop(0, 4, half_first)
    over_slab(2)
    share(1)
    pass_on(0)
    loop(0, 4, lambda i: next_yx(1, i))
    over_slab(3)
    share(2)
    pass_on(1)
    loop(0, 4, half_second)
    share(3)
    pass_on(2)
    loop(0, 4, lambda i: next_xy(1, i))

    def own_column(i):
        @pl.when(i == 1)
        def _():
            pass_on(3)
            loop(0, 4, lambda a: arrived(cols.at[q_core, :, a], COL_CORE + a))

        @pl.when(i == 3)
        def _():
            loop(0, 4, lambda a: arrived(cols.at[q_far, :, a], COL_FWD + a))

        second_project(jnp.where(i == 0, q, jnp.where(i == 1, q_x, jnp.where(i == 2, q_core, q_far))))

    loop(0, 4, own_column)

    finish(1)
    make_bias(1)

    def out_pass_on(c):
        block = outs.at[c, q_x]
        arrived(block, OUT_X + c)
        send(block, block, LEFT_OUT, OUT_FWD + c, other_core)
        out[pl.ds(4 * q_x + c, 128, stride=16), :] = outs[c, q_x]
        arrived(outs.at[c, q_core], OUT_CORE + c)
        out[pl.ds(4 * q_core + c, 128, stride=16), :] = outs[c, q_core]

    def second_attend(c):
        result = attend(c, 1)
        outs[c, q] = result
        block = outs.at[c, q]
        send(block, block, LEFT_OUT, OUT_X + c, other_x)
        send(block, block, LEFT_OUT, OUT_CORE + c, other_core)
        out[pl.ds(4 * q + c, 128, stride=16), :] = result

    loop(0, 4, second_attend)
    loop(0, 4, out_pass_on)

    def out_end(c):
        arrived(outs.at[c, q_far], OUT_FWD + c)
        out[pl.ds(4 * q_far + c, 128, stride=16), :] = outs[c, q_far]

    loop(0, 4, out_end)

    left(small.at[0:3], LEFT_SMALL)
    left(wp.at[0:3], LEFT_W)
    for layer in range(2):
        left(planes[layer].at[0:15, 0, 0], LEFT_Z[layer])
        left(planes[layer].at[0:14], LEFT_YX[layer])
    left(mid.at[:, 0:15], LEFT_PAIR_Z)
    left(mid2.at[:, 0:7], LEFT_PAIR_S)
    left(cols.at[0:3], LEFT_COL)
    left(outs.at[0:3], LEFT_OUT)


def shards(pair_rep, residue_mask, chain_ids, ln_gain, ln_shift, w_proj, w_bias, chain_bias, w_out):
    vmem = pl.BlockSpec(memory_space=pltpu.VMEM)
    hbm = pl.BlockSpec(memory_space=pltpu.HBM)
    result = pl.pallas_call(
        kernel,
        out_shape=jax.ShapeDtypeStruct((2048, 128), F32),
        in_specs=[hbm] * 9,
        out_specs=vmem,
        scratch_shapes=[
            pltpu.VMEM((4, 512, 128), F32),
            pltpu.VMEM((1, 512), jnp.int32),
            pltpu.VMEM((1, 512), jnp.int32),
            pltpu.VMEM((2, 128), F32),
            pltpu.VMEM((2, 128), F32),
            pltpu.VMEM((2, 128), F32),
            pltpu.VMEM((1, 2), F32),
            pltpu.VMEM((2, 128, 128), F32),
            pltpu.VMEM((4, 4, 128, 128), F32),
            pltpu.VMEM((4, 2, 128, 128), F32),
            pltpu.VMEM((4, 8, 128), F32),
            pltpu.VMEM((16, 4, 2, 16, 128), F32),
            pltpu.VMEM((16, 4, 2, 16, 128), F32),
            pltpu.VMEM((4, 128, 128), F32),
            pltpu.VMEM((4, 16, 8, 128), F32),
            pltpu.VMEM((4, 8, 16, 128), F32),
            pltpu.VMEM((4, 8, 4, 16, 128), F32),
            pltpu.VMEM((4, 4, 96, 512), BF16),
            pltpu.VMEM((4, 4, 96, 128), BF16),
            pltpu.VMEM((4, 4, 80, 512), BF16),
            pltpu.VMEM((4, 128, 128), F32),
            pltpu.VMEM((4, 128, 512), F32),
            pltpu.VMEM((256, 256), BF16),
            pltpu.VMEM((256, 256), BF16),
            pltpu.VMEM((2, 384, 128), BF16),
            pltpu.VMEM((8, 128), F32),
            pltpu.VMEM((4, 4, 128, 128), F32),
            pltpu.SemaphoreType.DMA((leave.count,)),
            pltpu.SemaphoreType.DMA((arrive.count,)),
        ],
        compiler_params=pltpu.CompilerParams(
            collective_id=0, has_side_effects=True, vmem_limit_bytes=40 * 1024 * 1024
        ),
    )(
        *(
            pltpu.with_memory_space_constraint(operand, pltpu.HBM)
            for operand in (
                pair_rep,
                residue_mask.reshape(1, 512),
                chain_ids.reshape(1, 512),
                ln_gain,
                ln_shift,
                w_proj.reshape(2, 128, 128),
                w_bias.reshape(2, 128),
                chain_bias.reshape(1, 2),
                w_out,
            )
        )
    )
    return result.reshape(512, 4, 128)


def solution(mesh):
    in_specs = (
        P("row", None, None),
        P(),
        P(),
        P(),
        P(),
        P(None, None, "head", None),
        P(None, None, "head"),
        P(None, "head"),
        P(),
    )
    return jax.shard_map(shards, mesh=mesh, in_specs=in_specs, out_specs=P(None, "row", None), check_vma=False)
```
